512 devices in a mesh: chan: 64 (over z_hi, y, x), freq: 8 (over z_lo, core).
Axes of the slice: x: 4, y: 8, z: 8 (z_hi: 2, z_lo: 4; z = z_hi * 4 + z_lo), core: 2. Of those that a mesh axis runs over, the one named last changes fastest.
Arguments:
- spectra: bfloat16 [16384, 64, 128], P('chan', 'freq'), may hold values from -6 to 6
- half_width: int32 [16384], P('chan'), may hold values from 1 to 4, as said below
- partners: int32 [3, 64], replicated, may hold values from 0 to 63, as said below
Outputs:
- correlations: bfloat16 [8, 4, 16384, 256], P('freq', None, 'chan')
The draws below stay inside these ranges and needn't reach their ends.
Inputs may be any that keep to these rules, and one draw needn't show every extreme that they name: partners[r, i] = i XOR m_r, where the 3 round masks m_r are distinct and lie in 1 .. 63. `half_width`: some channel has exactly 4.
All inputs are finite; a program needn't handle non-finite values.
Results may differ from the reference program's by a relative error of at most 0.017.
Values may be sent and summed in bfloat16 or wider, within the bound.
No kernel may reach another device: no remote copies, remote signals or barrier semaphores. Data moves between devices by JAX's collectives and lax.ppermute only.
A program may use at most 64 MiB of HBM per device.

```python
import jax
import jax.numpy as jnp
from jax import lax

CH_DEV = 256
BIN_DEV = 8
SEG = 64
HMAX = 4
ROUNDS = 3
PAIRS = 4
BLOCKS = 64
CHANNELS = 16384
BINS = 64
LAGS = 8
N_FREQ = 8


def draw_partners(key, part):
    key = jax.random.fold_in(key, 11)
    round_masks = jax.random.permutation(key, BLOCKS - 1)[:ROUNDS] + 1
    blocks_row = jnp.arange(BLOCKS, dtype=jnp.int32)[None, :]
    return jnp.bitwise_xor(blocks_row, round_masks.astype(jnp.int32)[:, None])


def draw_half_width(key, part):
    key = jax.random.fold_in(key, 23)
    first_key, second_key = jax.random.split(key)
    widths = jax.random.randint(first_key, (CHANNELS,), 1, HMAX + 1)
    position = jax.random.randint(second_key, (), 0, CHANNELS)
    return widths.at[position].set(HMAX).astype(jnp.int32)


def block_scale(key, shape, shards, least, top_value):
    gain, own = 1.0, jax.random.fold_in(key, 6)
    for axis_at, parts in shards:
        draws = jnp.exp(jax.random.uniform(jax.random.fold_in(own, axis_at), (parts,), jnp.float32, least / len(shards), top_value / len(shards)))
        gain = gain * jnp.repeat(draws, shape[axis_at] // parts).reshape([-1 if axis == axis_at else 1 for axis in range(len(shape))])
    return gain


def noise(own_key, extent, deviation, most, pieces=(), kind=jnp.bfloat16):
    entries = jax.random.normal(own_key, extent, jnp.float32) * deviation
    if len(pieces) > 0:
        entries = block_scale(own_key, extent, pieces, -0.22, 0.18) * entries
    return jnp.clip(entries, min=-most, max=most).astype(kind)


def setup_inputs(seed: int = 0) -> dict:
    seeds = jax.random.split(jax.random.key(seed), 4)
    return {
        "spectra": noise(seeds[0], (CHANNELS, BINS, 2 * SEG), 1.0, 6.0, ((0, 64), (1, 8))),
        "half_width": draw_half_width(jax.random.fold_in(seeds[3], 71), 0),
        "partners": draw_partners(jax.random.fold_in(seeds[3], 71), 0),
    }


def whiten(spectra, half_width):
    seg_count = spectra.shape[-1] // 2
    bin_count = spectra.shape[1]
    widened = spectra.astype(jnp.float32)
    powers = widened[..., :seg_count] ** 2 + widened[..., seg_count:] ** 2
    padded = jnp.pad(powers, ((0, 0), (HMAX, HMAX), (0, 0)))
    window_sum = jnp.zeros_like(powers)
    for offset in range(-HMAX, HMAX + 1):
        window = padded[:, HMAX + offset:HMAX + offset + bin_count]
        window_sum = window_sum + jnp.where(abs(offset) <= half_width[:, None, None], window, jnp.float32(0.0))
    smooth = window_sum / (2 * half_width + 1).astype(jnp.float32)[:, None, None]
    inverse = lax.rsqrt(jnp.maximum(smooth, jnp.float32(0.5)))
    return (widened * jnp.concatenate([inverse, inverse], -1)).astype(jnp.bfloat16)

def cross_pair(left_block, right_block):
    seg_count = left_block.shape[-1] // 2
    left_wide = left_block.astype(jnp.float32)
    right_wide = right_block.astype(jnp.float32)
    turned = jnp.concatenate([left_wide[..., seg_count:], -left_wide[..., :seg_count]], -1)
    real_part = jnp.einsum('agk,bgk->gab', left_wide, right_wide, precision=lax.Precision.HIGHEST)
    imag_part = jnp.einsum('agk,bgk->gab', turned, right_wide, precision=lax.Precision.HIGHEST)
    return (real_part, imag_part)

def reference(spectra, half_width, partners):
    white = whiten(spectra, half_width)
    bin_index = jnp.arange(BINS, dtype=jnp.float32)
    lag_index = jnp.arange(LAGS, dtype=jnp.float32)
    theta = 2.0 * jnp.pi * bin_index[:, None] * lag_index[None, :] / BINS
    factor = 1.0 / jnp.sqrt(jnp.float32(SEG * BINS))
    cosine = (jnp.cos(theta) * factor).reshape(N_FREQ, BIN_DEV, LAGS)
    sine_table = (jnp.sin(theta) * factor).reshape(N_FREQ, BIN_DEV, LAGS)

    def one_block(block_index):
        mine = lax.dynamic_slice_in_dim(white, block_index * CH_DEV, CH_DEV, 0)
        results = []
        for pair_index in range(PAIRS):
            if pair_index == 0:
                partner_index = block_index
            else:
                partner_index = partners[pair_index - 1, block_index].astype(jnp.int32)
            partner_block = lax.dynamic_slice_in_dim(white, partner_index * CH_DEV, CH_DEV, 0)
            real_part, imag_part = cross_pair(mine, partner_block)
            real_slices = real_part.reshape(N_FREQ, BIN_DEV, CH_DEV, CH_DEV)
            imag_slices = imag_part.reshape(N_FREQ, BIN_DEV, CH_DEV, CH_DEV)
            partial_value = jnp.einsum('qgab,qgl->qlab', real_slices, cosine, precision=lax.Precision.HIGHEST)
            partial_value = partial_value - jnp.einsum('qgab,qgl->qlab', imag_slices, sine_table, precision=lax.Precision.HIGHEST)
            rounded = lax.optimization_barrier(partial_value.astype(jnp.bfloat16))
            results.append(lax.optimization_barrier(jnp.sum(rounded.astype(jnp.float32), 0)))
        return jnp.stack(results, 1).astype(jnp.bfloat16)
    stacked = lax.map(one_block, jnp.arange(BLOCKS, dtype=jnp.int32))
    return stacked.transpose(1, 2, 0, 3, 4).reshape(LAGS, PAIRS, CHANNELS, CH_DEV)
```

```python
import functools

import jax
import jax.numpy as jnp
import numpy as np
from jax import lax
from jax.experimental import pallas as pl
from jax.experimental.pallas import tpu as pltpu
from jax.sharding import PartitionSpec as P

HMAX = 4
ROUNDS = 3
CORES = 2
ROWS = 16
ORDER = (0, 2, 1, 3)
NEAR = 4


def tables(freq_count, bin_dev, seg_count):
    chips = freq_count // CORES
    bin_count = freq_count * bin_dev
    out = np.zeros((freq_count, 2 * chips, CORES * bin_dev, 2 * seg_count), np.float32)
    sign = np.where(np.arange(2 * seg_count) < seg_count, -1.0, 1.0)
    for index in range(freq_count):
        chip, core = index // CORES, index % CORES
        bins = np.concatenate(
            [index * bin_dev + np.arange(bin_dev), (index ^ 1) * bin_dev + np.arange(bin_dev)]
        )
        for d in range(chips):
            lag = (chip ^ ORDER[d]) * CORES + core
            theta = 2.0 * np.pi * ((bins * lag) % bin_count) / bin_count
            factor = 1.0 / np.sqrt(seg_count * bin_count)
            out[index, d] = np.cos(theta)[:, None] * factor
            out[index, chips + d] = np.sin(theta)[:, None] * factor * sign
    return out.reshape(freq_count, 2 * chips, -1)


def whiten_kernel(bin_dev, width, x_ref, low_ref, high_ref, half_ref, out_ref):
    half = width // 2

    def block(ref, rows, index):
        return ref[rows, index * width : (index + 1) * width].astype(jnp.float32)

    def step(i, carry):
        rows = pl.ds(pl.multiple_of(i * ROWS, ROWS), ROWS)
        own = [block(x_ref, rows, g) for g in range(bin_dev)]
        wide = [block(low_ref, rows, g) for g in range(HMAX)]
        wide += own
        wide += [block(high_ref, rows, g) for g in range(HMAX)]
        power = []
        for value in wide:
            square = value * value
            power.append(square + pltpu.roll(square, half, 1))
        hw = half_ref[rows, :]
        scale = 1.0 / (2.0 * hw + 1.0)
        for g in range(bin_dev):
            centre = g + HMAX
            total = power[centre]
            for k in range(1, HMAX + 1):
                both = power[centre - k] + power[centre + k]
                total = total + (both if k == 1 else jnp.where(hw >= k, both, 0.0))
            smooth = jnp.maximum(total * scale, 0.5)
            out_ref[rows, g * width : (g + 1) * width] = (own[g] * lax.rsqrt(smooth)).astype(
                jnp.bfloat16
            )
        return carry

    lax.fori_loop(0, x_ref.shape[0] // ROWS, step, 0)


def whiten(x, low, high, half_wide, bin_dev):
    return pl.pallas_call(
        functools.partial(whiten_kernel, bin_dev, x.shape[1] // bin_dev),
        out_shape=jax.ShapeDtypeStruct(x.shape, jnp.bfloat16),
        compiler_params=pltpu.CompilerParams(vmem_limit_bytes=16 << 20),
        name="whiten",
    )(x, low, high, half_wide)


NT = (((1,), (1,)), ((), ()))


def correlate(turned_ref, blocks, out_ref):
    def step(d, carry):
        for j, (mine_ref, other_ref) in enumerate(blocks):
            span = mine_ref.shape[1]
            total = lax.dot_general(
                turned_ref[d, :, :span], mine_ref[...], NT, preferred_element_type=jnp.float32
            )
            total += lax.dot_general(
                turned_ref[d, :, span:], other_ref[...], NT, preferred_element_type=jnp.float32
            )
            out_ref[d, j] = total.astype(jnp.bfloat16)
        return carry

    lax.fori_loop(0, turned_ref.shape[0], step, 0)


def first_kernel(width, mine_ref, other_ref, table_ref, turned_ref, out_ref):
    rows_all, span = mine_ref.shape
    chips = turned_ref.shape[0]
    for part, ref in enumerate((mine_ref, other_ref)):

        def turn(g, carry, part=part, ref=ref):
            lanes = pl.ds(pl.multiple_of(g * width, width), width)
            to = pl.ds(pl.multiple_of(part * span + g * width, width), width)
            wide = [jnp.broadcast_to(table_ref[k : k + 1, to], (ROWS, width)) for k in range(2 * chips)]

            def step(i, inner):
                rows = pl.ds(pl.multiple_of(i * ROWS, ROWS), ROWS)
                value = ref[rows, lanes].astype(jnp.float32)
                swapped = pltpu.roll(value, width // 2, 1)
                for d in range(chips):
                    turned_ref[d, rows, to] = (value * wide[d] + swapped * wide[chips + d]).astype(
                        jnp.bfloat16
                    )
                return inner

            return lax.fori_loop(0, rows_all // ROWS, step, carry, unroll=8)

        lax.fori_loop(0, span // width, turn, 0)
    correlate(turned_ref, [(mine_ref, other_ref)], out_ref)


def first_pair(mine, other, table, width):
    rows, span = mine.shape
    chips = table.shape[0] // 2
    return pl.pallas_call(
        functools.partial(first_kernel, width),
        out_shape=[
            jax.ShapeDtypeStruct((chips, rows, 2 * span), jnp.bfloat16),
            jax.ShapeDtypeStruct((chips, 1, rows, rows), jnp.bfloat16),
        ],
        compiler_params=pltpu.CompilerParams(vmem_limit_bytes=20 << 20),
        name="first_pair",
    )(mine, other, table)


def pairs_kernel(turned_ref, *refs):
    correlate(turned_ref, list(zip(refs[:-1:2], refs[1:-1:2])), refs[-1])


def next_pairs(turned, *halves):
    rows = halves[0].shape[0]
    return pl.pallas_call(
        pairs_kernel,
        out_shape=jax.ShapeDtypeStruct(
            (turned.shape[0], len(halves) // 2, rows, rows), jnp.bfloat16
        ),
        compiler_params=pltpu.CompilerParams(vmem_limit_bytes=20 << 20),
        cost_estimate=pl.CostEstimate(
            flops=2 * len(halves) * turned.size * rows, bytes_accessed=2 * turned.size, transcendentals=0
        ),
        name="next_pairs",
    )(turned, *halves)


def swap_cores(block, size):
    return lax.ppermute(block, "freq", [(i, i ^ 1) for i in range(size)])


def scatter(partial, size):
    kept = partial.shape[0] // 2
    beside = [(i, i ^ CORES) for i in range(size)]
    across = [(i, i ^ (2 * CORES)) for i in range(size)]
    arrived = lax.ppermute(partial[kept:], "freq", beside).astype(jnp.float32)
    passing = (partial[1].astype(jnp.float32) + arrived[1]).astype(jnp.bfloat16)
    passed = lax.ppermute(passing, "freq", across).astype(jnp.float32)
    return (partial[0].astype(jnp.float32) + arrived[0] + passed).astype(jnp.bfloat16)


def exchange(block, mask, count):
    if mask == 0:
        return block
    return lax.ppermute(block, "chan", [(i, i ^ mask) for i in range(count)])


def far_side(left, right, count):
    half = left.shape[0] // 2
    return exchange(left[:half], 3, count), exchange(right[half:], 1, count)


def pick_kernel(mask_ref, own, left, right, low_part, high_part, *refs):
    outs, sems = refs[:-1], refs[-1]
    half = own.shape[0] // 2
    for r, out in enumerate(outs):
        near = mask_ref[r, 0] & (NEAR - 1)
        lower, upper = out.at[pl.ds(0, half)], out.at[pl.ds(half, half)]
        for value, block in ((0, own), (1, left), (3, right)):

            @pl.when(near == value)
            def _(block=block, lower=lower, upper=upper, r=r):
                pltpu.make_async_copy(block.at[pl.ds(0, half)], lower, sems.at[r, 0]).start()
                pltpu.make_async_copy(block.at[pl.ds(half, half)], upper, sems.at[r, 1]).start()

        @pl.when(near == 2)
        def _(lower=lower, upper=upper, r=r):
            pltpu.make_async_copy(low_part, lower, sems.at[r, 0]).start()
            pltpu.make_async_copy(high_part, upper, sems.at[r, 1]).start()

    for r, out in enumerate(outs):
        pltpu.make_async_copy(low_part, out.at[pl.ds(0, half)], sems.at[r, 0]).wait()
        pltpu.make_async_copy(high_part, out.at[pl.ds(half, half)], sems.at[r, 1]).wait()


def pick(partners, own, *pieces):
    return pl.pallas_call(
        pick_kernel,
        in_specs=[pl.BlockSpec(memory_space=pltpu.SMEM)]
        + [pl.BlockSpec(memory_space=pl.ANY)] * (1 + len(pieces)),
        out_specs=[pl.BlockSpec(memory_space=pl.ANY)] * ROUNDS,
        out_shape=[jax.ShapeDtypeStruct(own.shape, own.dtype)] * ROUNDS,
        scratch_shapes=[pltpu.SemaphoreType.DMA((ROUNDS, 2))],
        compiler_params=pltpu.CompilerParams(vmem_limit_bytes=1 << 20),
        name="pick",
    )(partners, own, *pieces)


def shards(spectra, half_width, partners):
    freq_count = lax.axis_size("freq")
    chan_count = lax.axis_size("chan")
    channels, bin_dev, width = spectra.shape
    far_count = chan_count // NEAR
    x = spectra.reshape(channels, bin_dev * width)
    edge = HMAX * width
    up = [(i, i + 1) for i in range(freq_count - 1)]
    down = [(i + 1, i) for i in range(freq_count - 1)]
    low = lax.ppermute(x[:, -edge:], "freq", up)
    high = lax.ppermute(x[:, :edge], "freq", down)
    half_wide = jnp.broadcast_to(half_width.astype(jnp.float32)[:, None], (channels, width))
    table = lax.dynamic_index_in_dim(
        jnp.asarray(tables(freq_count, bin_dev, width // 2)),
        lax.axis_index("freq"),
        0,
        keepdims=False,
    )
    white = whiten(x, low, high, half_wide, bin_dev)
    left, right = exchange(white, 1, chan_count), exchange(white, 3, chan_count)
    other = swap_cores(white, freq_count)
    turned, partial = first_pair(white, other, table, width)
    left, right, partial = lax.optimization_barrier((left, right, partial))
    picked = pick(partners, white, left, right, *far_side(left, right, chan_count))
    far = partners[:, 0] >> (NEAR.bit_length() - 1)
    *picked, partial = lax.optimization_barrier((*picked, partial))

    def first_stage(mask):
        def run(block, partial):
            return exchange(block, mask * NEAR, chan_count), scatter(partial, freq_count)

        return run

    def second_stage(mask):
        def run(block, held):
            return exchange(block, mask * NEAR, chan_count), swap_cores(held, freq_count)

        return run

    def last_stage(mask):
        def run(block, held, partial):
            arriving = exchange(block, mask * NEAR, chan_count)
            return arriving, swap_cores(held, freq_count), scatter(partial, freq_count)

        return run

    def stage(make, r, *operands):
        return lax.switch(far[r], [make(k) for k in range(far_count)], *operands)

    block_0, sum_own = stage(first_stage, 0, picked[0], partial)
    block_1, other_0 = stage(second_stage, 1, picked[1], block_0)
    partial = next_pairs(turned, block_0, other_0)
    block_2, other_1, sum_0 = stage(last_stage, 2, picked[2], block_1, partial)
    sum_1 = scatter(next_pairs(turned, block_1, other_1), freq_count)
    partial = next_pairs(turned, block_2, swap_cores(block_2, freq_count))
    return jnp.concatenate([sum_own, sum_0, sum_1, scatter(partial, freq_count)])[None]


def solution(mesh):
    return jax.shard_map(
        shards,
        mesh=mesh,
        in_specs=(P("chan", "freq", None), P("chan"), P()),
        out_specs=P("freq", None, "chan", None),
        check_vma=False,
    )
```

```python
import functools

import jax
import jax.numpy as jnp
import numpy as np
from jax import lax
from jax.experimental import pallas as pl
from jax.experimental.pallas import tpu as pltpu
from jax.sharding import PartitionSpec as P

HMAX = 4
ROUNDS = 3
CORES = 2
ROWS = 16
ORDER = (0, 2, 1, 3)
NEAR = 4


def tables(freq_count, bin_dev, seg_count):
    chips = freq_count // CORES
    bin_count = freq_count * bin_dev
    out = np.zeros((freq_count, 2 * chips, CORES * bin_dev, 2 * seg_count), np.float32)
    sign = np.where(np.arange(2 * seg_count) < seg_count, -1.0, 1.0)
    for index in range(freq_count):
        chip, core = index // CORES, index % CORES
        bins = np.concatenate(
            [index * bin_dev + np.arange(bin_dev), (index ^ 1) * bin_dev + np.arange(bin_dev)]
        )
        for d in range(chips):
            lag = (chip ^ ORDER[d]) * CORES + core
            theta = 2.0 * np.pi * ((bins * lag) % bin_count) / bin_count
            factor = 1.0 / np.sqrt(seg_count * bin_count)
            out[index, d] = np.cos(theta)[:, None] * factor
            out[index, chips + d] = np.sin(theta)[:, None] * factor * sign
    return out.reshape(freq_count, 2 * chips, -1)


def whiten_kernel(bin_dev, width, x_ref, low_ref, high_ref, half_ref, out_ref):
    half = width // 2

    def block(ref, rows, index):
        return ref[rows, index * width : (index + 1) * width].astype(jnp.float32)

    def step(i, carry):
        rows = pl.ds(pl.multiple_of(i * ROWS, ROWS), ROWS)
        own = [block(x_ref, rows, g) for g in range(bin_dev)]
        wide = [block(low_ref, rows, g) for g in range(HMAX)]
        wide += own
        wide += [block(high_ref, rows, g) for g in range(HMAX)]
        power = []
        for value in wide:
            square = value * value
            power.append(square + pltpu.roll(square, half, 1))
        hw = half_ref[rows, :]
        scale = 1.0 / (2.0 * hw + 1.0)
        for g in range(bin_dev):
            centre = g + HMAX
            total = power[centre]
            for k in range(1, HMAX + 1):
                both = power[centre - k] + power[centre + k]
                total = total + (both if k == 1 else jnp.where(hw >= k, both, 0.0))
            smooth = jnp.maximum(total * scale, 0.5)
            out_ref[rows, g * width : (g + 1) * width] = (own[g] * lax.rsqrt(smooth)).astype(
                jnp.bfloat16
            )
        return carry

    lax.fori_loop(0, x_ref.shape[0] // ROWS, step, 0)


def whiten(x, low, high, half_wide, bin_dev):
    return pl.pallas_call(
        functools.partial(whiten_kernel, bin_dev, x.shape[1] // bin_dev),
        out_shape=jax.ShapeDtypeStruct(x.shape, jnp.bfloat16),
        compiler_params=pltpu.CompilerParams(vmem_limit_bytes=16 << 20),
        name="whiten",
    )(x, low, high, half_wide)


NT = (((1,), (1,)), ((), ()))


def correlate(turned_ref, blocks, out_ref):
    def step(d, carry):
        for j, (mine_ref, other_ref) in enumerate(blocks):
            span = mine_ref.shape[1]
            total = lax.dot_general(
                turned_ref[d, :, :span], mine_ref[...], NT, preferred_element_type=jnp.float32
            )
            total += lax.dot_general(
                turned_ref[d, :, span:], other_ref[...], NT, preferred_element_type=jnp.float32
            )
            out_ref[d, j] = total.astype(jnp.bfloat16)
        return carry

    lax.fori_loop(0, turned_ref.shape[0], step, 0)


def first_kernel(width, mine_ref, other_ref, table_ref, turned_ref, out_ref):
    rows_all, span = mine_ref.shape
    chips = turned_ref.shape[0]
    for part, ref in enumerate((mine_ref, other_ref)):

        def turn(g, carry, part=part, ref=ref):
            lanes = pl.ds(pl.multiple_of(g * width, width), width)
            to = pl.ds(pl.multiple_of(part * span + g * width, width), width)
            wide = [jnp.broadcast_to(table_ref[k : k + 1, to], (ROWS, width)) for k in range(2 * chips)]

            def step(i, inner):
                rows = pl.ds(pl.multiple_of(i * ROWS, ROWS), ROWS)
                value = ref[rows, lanes].astype(jnp.float32)
                swapped = pltpu.roll(value, width // 2, 1)
                for d in range(chips):
                    turned_ref[d, rows, to] = (value * wide[d] + swapped * wide[chips + d]).astype(
                        jnp.bfloat16
                    )
                return inner

            return lax.fori_loop(0, rows_all // ROWS, step, carry, unroll=8)

        lax.fori_loop(0, span // width, turn, 0)
    correlate(turned_ref, [(mine_ref, other_ref)], out_ref)


def first_pair(mine, other, table, width):
    rows, span = mine.shape
    chips = table.shape[0] // 2
    return pl.pallas_call(
        functools.partial(first_kernel, width),
        out_shape=[
            jax.ShapeDtypeStruct((chips, rows, 2 * span), jnp.bfloat16),
            jax.ShapeDtypeStruct((chips, 1, rows, rows), jnp.bfloat16),
        ],
        compiler_params=pltpu.CompilerParams(vmem_limit_bytes=20 << 20),
        name="first_pair",
    )(mine, other, table)


def pairs_kernel(turned_ref, *refs):
    correlate(turned_ref, list(zip(refs[:-1:2], refs[1:-1:2])), refs[-1])


def next_pairs(turned, *halves):
    rows = halves[0].shape[0]
    return pl.pallas_call(
        pairs_kernel,
        out_shape=jax.ShapeDtypeStruct(
            (turned.shape[0], len(halves) // 2, rows, rows), jnp.bfloat16
        ),
        compiler_params=pltpu.CompilerParams(vmem_limit_bytes=20 << 20),
        cost_estimate=pl.CostEstimate(
            flops=2 * len(halves) * turned.size * rows, bytes_accessed=2 * turned.size, transcendentals=0
        ),
        name="next_pairs",
    )(turned, *halves)


def swap_cores(block, size):
    return lax.ppermute(block, "freq", [(i, i ^ 1) for i in range(size)])


def beside_step(partial, size):
    half = partial.shape[0] // 2
    route = [(i, i ^ CORES) for i in range(size)]
    arrived = lax.ppermute(partial[half:], "freq", route).astype(jnp.float32)
    passing = (partial[1].astype(jnp.float32) + arrived[1]).astype(jnp.bfloat16)
    return partial[0].astype(jnp.float32) + arrived[0], passing


def across_step(kept, passing, size):
    route = [(i, i ^ (2 * CORES)) for i in range(size)]
    passed = lax.ppermute(passing, "freq", route).astype(jnp.float32)
    return (kept + passed).astype(jnp.bfloat16)


def scatter(partial, size):
    return across_step(*beside_step(partial, size), size)


def exchange(block, mask, count):
    if mask == 0:
        return block
    return lax.ppermute(block, "chan", [(i, i ^ mask) for i in range(count)])


def pick_kernel(top, mask_ref, own, far, *refs):
    outs, sems = refs[:-1], refs[-1]
    for r, out in enumerate(outs):
        high = mask_ref[r, 0] & top

        @pl.when(high == 0)
        def _(out=out, r=r):
            pltpu.make_async_copy(own, out, sems.at[r]).start()

        @pl.when(high != 0)
        def _(out=out, r=r):
            pltpu.make_async_copy(far, out, sems.at[r]).start()

    for r, out in enumerate(outs):
        pltpu.make_async_copy(own, out, sems.at[r]).wait()


def pick(partners, own, far, top):
    return pl.pallas_call(
        functools.partial(pick_kernel, top),
        in_specs=[pl.BlockSpec(memory_space=pltpu.SMEM)] + [pl.BlockSpec(memory_space=pl.ANY)] * 2,
        out_specs=[pl.BlockSpec(memory_space=pl.ANY)] * ROUNDS,
        out_shape=[jax.ShapeDtypeStruct(own.shape, own.dtype)] * ROUNDS,
        scratch_shapes=[pltpu.SemaphoreType.DMA((ROUNDS,))],
        compiler_params=pltpu.CompilerParams(vmem_limit_bytes=1 << 20),
        name="pick",
    )(partners, own, far)


def shards(spectra, half_width, partners):
    freq_count = lax.axis_size("freq")
    chan_count = lax.axis_size("chan")
    channels, bin_dev, width = spectra.shape
    x = spectra.reshape(channels, bin_dev * width)
    edge = HMAX * width
    up = [(i, i + 1) for i in range(freq_count - 1)]
    down = [(i + 1, i) for i in range(freq_count - 1)]
    low = lax.ppermute(x[:, -edge:], "freq", up)
    high = lax.ppermute(x[:, :edge], "freq", down)
    half_wide = jnp.broadcast_to(half_width.astype(jnp.float32)[:, None], (channels, width))
    table = lax.dynamic_index_in_dim(
        jnp.asarray(tables(freq_count, bin_dev, width // 2)),
        lax.axis_index("freq"),
        0,
        keepdims=False,
    )
    white = whiten(x, low, high, half_wide, bin_dev)
    top = chan_count // 2
    far_white = exchange(white, top, chan_count)
    other = swap_cores(white, freq_count)
    turned, partial = first_pair(white, other, table, width)
    far_white, partial = lax.optimization_barrier((far_white, partial))
    base = pick(partners, white, far_white, top)
    masks = partners[:, 0]
    x_of, y_of = masks & (NEAR - 1), (masks & (top - 1)) >> (NEAR.bit_length() - 1)
    y_count = top // NEAR

    def stage(y_round, y_block, x_round, x_block, beside, *operands):
        def make(y_mask, x_mask):
            def run(y_block, x_block, *operands):
                return (
                    exchange(y_block, y_mask * NEAR, chan_count),
                    exchange(x_block, x_mask, chan_count),
                    beside(*operands),
                )

            return run

        return lax.switch(
            y_of[y_round] * NEAR + x_of[x_round],
            [make(i, j) for i in range(y_count) for j in range(NEAR)],
            y_block,
            x_block,
            *operands,
        )

    half_0, half_1, _ = stage(0, base[0], 1, base[1], lambda: ())
    kept, passing = beside_step(partial, freq_count)
    half_0, half_1, kept, passing = lax.optimization_barrier((half_0, half_1, kept, passing))
    block_1, half_2, sum_own = stage(
        1, half_1, 2, base[2], lambda *sums: across_step(*sums, freq_count), kept, passing
    )
    block_2, block_0, other_1 = stage(
        2, half_2, 0, half_0, lambda block: swap_cores(block, freq_count), block_1
    )
    sum_1 = scatter(next_pairs(turned, block_1, other_1), freq_count)
    other_0, other_2 = swap_cores(block_0, freq_count), swap_cores(block_2, freq_count)
    sum_02 = scatter(next_pairs(turned, block_0, other_0, block_2, other_2), freq_count)
    return jnp.concatenate([sum_own, sum_02[:1], sum_1, sum_02[1:]])[None]


def solution(mesh):
    return jax.shard_map(
        shards,
        mesh=mesh,
        in_specs=(P("chan", "freq", None), P("chan"), P()),
        out_specs=P("freq", None, "chan", None),
        check_vma=False,
    )
```

```python
import functools

import jax
import jax.numpy as jnp
import numpy as np
from jax import lax
from jax.experimental import pallas as pl
from jax.experimental.pallas import tpu as pltpu
from jax.sharding import PartitionSpec as P

HMAX = 4
ROUNDS = 3
CORES = 2
ROWS = 16
ORDER = (0, 2, 1, 3)
NEAR = 4


def tables(freq_count, bin_dev, seg_count):
    chips = freq_count // CORES
    bin_count = freq_count * bin_dev
    out = np.zeros((freq_count, 2 * chips, CORES * bin_dev, 2 * seg_count), np.float32)
    sign = np.where(np.arange(2 * seg_count) < seg_count, -1.0, 1.0)
    for index in range(freq_count):
        chip, core = index // CORES, index % CORES
        bins = np.concatenate(
            [index * bin_dev + np.arange(bin_dev), (index ^ 1) * bin_dev + np.arange(bin_dev)]
        )
        for d in range(chips):
            lag = (chip ^ ORDER[d]) * CORES + core
            theta = 2.0 * np.pi * ((bins * lag) % bin_count) / bin_count
            factor = 1.0 / np.sqrt(seg_count * bin_count)
            out[index, d] = np.cos(theta)[:, None] * factor
            out[index, chips + d] = np.sin(theta)[:, None] * factor * sign
    return out.reshape(freq_count, 2 * chips, -1)


def whiten_kernel(bin_dev, width, x_ref, low_ref, high_ref, half_ref, out_ref):
    half = width // 2

    def block(ref, rows, index):
        return ref[rows, index * width : (index + 1) * width].astype(jnp.float32)

    def step(i, carry):
        rows = pl.ds(pl.multiple_of(i * ROWS, ROWS), ROWS)
        own = [block(x_ref, rows, g) for g in range(bin_dev)]
        wide = [block(low_ref, rows, g) for g in range(HMAX)]
        wide += own
        wide += [block(high_ref, rows, g) for g in range(HMAX)]
        power = []
        for value in wide:
            square = value * value
            power.append(square + pltpu.roll(square, half, 1))
        hw = half_ref[rows, :]
        scale = 1.0 / (2.0 * hw + 1.0)
        for g in range(bin_dev):
            centre = g + HMAX
            total = power[centre]
            for k in range(1, HMAX + 1):
                both = power[centre - k] + power[centre + k]
                total = total + (both if k == 1 else jnp.where(hw >= k, both, 0.0))
            smooth = jnp.maximum(total * scale, 0.5)
            out_ref[rows, g * width : (g + 1) * width] = (own[g] * lax.rsqrt(smooth)).astype(
                jnp.bfloat16
            )
        return carry

    lax.fori_loop(0, x_ref.shape[0] // ROWS, step, 0)


def whiten(x, low, high, half_wide, bin_dev):
    return pl.pallas_call(
        functools.partial(whiten_kernel, bin_dev, x.shape[1] // bin_dev),
        out_shape=jax.ShapeDtypeStruct(x.shape, jnp.bfloat16),
        compiler_params=pltpu.CompilerParams(vmem_limit_bytes=16 << 20),
        name="whiten",
    )(x, low, high, half_wide)


NT = (((1,), (1,)), ((), ()))


def correlate(turned_ref, blocks, out_ref):
    def step(d, carry):
        for j, (mine_ref, other_ref) in enumerate(blocks):
            span = mine_ref.shape[1]
            total = lax.dot_general(
                turned_ref[d, :, :span], mine_ref[...], NT, preferred_element_type=jnp.float32
            )
            total += lax.dot_general(
                turned_ref[d, :, span:], other_ref[...], NT, preferred_element_type=jnp.float32
            )
            out_ref[d, j] = total.astype(jnp.bfloat16)
        return carry

    lax.fori_loop(0, turned_ref.shape[0], step, 0)


def first_kernel(width, mine_ref, other_ref, table_ref, turned_ref, out_ref):
    rows_all, span = mine_ref.shape
    chips = turned_ref.shape[0]
    for part, ref in enumerate((mine_ref, other_ref)):

        def turn(g, carry, part=part, ref=ref):
            lanes = pl.ds(pl.multiple_of(g * width, width), width)
            to = pl.ds(pl.multiple_of(part * span + g * width, width), width)
            wide = [jnp.broadcast_to(table_ref[k : k + 1, to], (ROWS, width)) for k in range(2 * chips)]

            def step(i, inner):
                rows = pl.ds(pl.multiple_of(i * ROWS, ROWS), ROWS)
                value = ref[rows, lanes].astype(jnp.float32)
                swapped = pltpu.roll(value, width // 2, 1)
                for d in range(chips):
                    turned_ref[d, rows, to] = (value * wide[d] + swapped * wide[chips + d]).astype(
                        jnp.bfloat16
                    )
                return inner

            return lax.fori_loop(0, rows_all // ROWS, step, carry, unroll=8)

        lax.fori_loop(0, span // width, turn, 0)
    correlate(turned_ref, [(mine_ref, other_ref)], out_ref)


def first_pair(mine, other, table, width):
    rows, span = mine.shape
    chips = table.shape[0] // 2
    return pl.pallas_call(
        functools.partial(first_kernel, width),
        out_shape=[
            jax.ShapeDtypeStruct((chips, rows, 2 * span), jnp.bfloat16),
            jax.ShapeDtypeStruct((chips, 1, rows, rows), jnp.bfloat16),
        ],
        compiler_params=pltpu.CompilerParams(vmem_limit_bytes=20 << 20),
        name="first_pair",
    )(mine, other, table)


def pairs_kernel(turned_ref, *refs):
    correlate(turned_ref, list(zip(refs[:-1:2], refs[1:-1:2])), refs[-1])


def next_pairs(turned, *halves):
    rows = halves[0].shape[0]
    return pl.pallas_call(
        pairs_kernel,
        out_shape=jax.ShapeDtypeStruct(
            (turned.shape[0], len(halves) // 2, rows, rows), jnp.bfloat16
        ),
        compiler_params=pltpu.CompilerParams(vmem_limit_bytes=20 << 20),
        cost_estimate=pl.CostEstimate(
            flops=2 * len(halves) * turned.size * rows, bytes_accessed=2 * turned.size, transcendentals=0
        ),
        name="next_pairs",
    )(turned, *halves)


def swap_cores(block, size):
    return lax.ppermute(block, "freq", [(i, i ^ 1) for i in range(size)])


def beside_step(partial, size):
    half = partial.shape[0] // 2
    route = [(i, i ^ CORES) for i in range(size)]
    arrived = lax.ppermute(partial[half:], "freq", route).astype(jnp.float32)
    passing = (partial[1].astype(jnp.float32) + arrived[1]).astype(jnp.bfloat16)
    return partial[0].astype(jnp.float32) + arrived[0], passing


def across_step(kept, passing, size):
    route = [(i, i ^ (2 * CORES)) for i in range(size)]
    passed = lax.ppermute(passing, "freq", route).astype(jnp.float32)
    return (kept + passed).astype(jnp.bfloat16)


def scatter(partial, size):
    return across_step(*beside_step(partial, size), size)


def exchange(block, mask, count):
    if mask == 0:
        return block
    return lax.ppermute(block, "chan", [(i, i ^ mask) for i in range(count)])


def along_z(block, step, chan_count, freq_count):
    chips, below = freq_count // CORES, chan_count // 2
    ring = 2 * chips

    def place(z, rest, core):
        return ((z // chips) * below + rest) * freq_count + (z % chips) * CORES + core

    route = [
        (place(z, rest, core), place((z + step) % ring, rest, core))
        for z in range(ring)
        for rest in range(below)
        for core in range(CORES)
    ]
    return lax.ppermute(block, ("chan", "freq"), route)


def pick_kernel(top, mask_ref, own, lower, upper, *refs):
    outs, sems = refs[:-1], refs[-1]
    half = lower.shape[0]
    for r, out in enumerate(outs):
        high = mask_ref[r, 0] & top
        first, second = out.at[pl.ds(0, half)], out.at[pl.ds(half, half)]

        @pl.when(high == 0)
        def _(first=first, second=second, r=r):
            pltpu.make_async_copy(own.at[pl.ds(0, half)], first, sems.at[r, 0]).start()
            pltpu.make_async_copy(own.at[pl.ds(half, half)], second, sems.at[r, 1]).start()

        @pl.when(high != 0)
        def _(first=first, second=second, r=r):
            pltpu.make_async_copy(lower, first, sems.at[r, 0]).start()
            pltpu.make_async_copy(upper, second, sems.at[r, 1]).start()

    for r, out in enumerate(outs):
        pltpu.make_async_copy(lower, out.at[pl.ds(0, half)], sems.at[r, 0]).wait()
        pltpu.make_async_copy(upper, out.at[pl.ds(half, half)], sems.at[r, 1]).wait()


def pick(partners, own, lower, upper, top):
    return pl.pallas_call(
        functools.partial(pick_kernel, top),
        in_specs=[pl.BlockSpec(memory_space=pltpu.SMEM)] + [pl.BlockSpec(memory_space=pl.ANY)] * 3,
        out_specs=[pl.BlockSpec(memory_space=pl.ANY)] * ROUNDS,
        out_shape=[jax.ShapeDtypeStruct(own.shape, own.dtype)] * ROUNDS,
        scratch_shapes=[pltpu.SemaphoreType.DMA((ROUNDS, 2))],
        compiler_params=pltpu.CompilerParams(vmem_limit_bytes=1 << 20),
        name="pick",
    )(partners, own, lower, upper)


def shards(spectra, half_width, partners):
    freq_count = lax.axis_size("freq")
    chan_count = lax.axis_size("chan")
    channels, bin_dev, width = spectra.shape
    x = spectra.reshape(channels, bin_dev * width)
    edge = HMAX * width
    up = [(i, i + 1) for i in range(freq_count - 1)]
    down = [(i + 1, i) for i in range(freq_count - 1)]
    low = lax.ppermute(x[:, -edge:], "freq", up)
    high = lax.ppermute(x[:, :edge], "freq", down)
    half_wide = jnp.broadcast_to(half_width.astype(jnp.float32)[:, None], (channels, width))
    table = lax.dynamic_index_in_dim(
        jnp.asarray(tables(freq_count, bin_dev, width // 2)),
        lax.axis_index("freq"),
        0,
        keepdims=False,
    )
    white = whiten(x, low, high, half_wide, bin_dev)
    top, half = chan_count // 2, channels // 2
    y_count = top // NEAR
    masks = partners[:, 0]
    x_of, y_of = masks & (NEAR - 1), (masks & (top - 1)) >> (NEAR.bit_length() - 1)
    index = [y_of[r] * NEAR + x_of[(r + 1) % ROUNDS] for r in range(ROUNDS)]
    hop = freq_count // CORES // 2
    lower = along_z(white[:half], hop, chan_count, freq_count)
    upper = along_z(white[half:], -hop, chan_count, freq_count)
    other, *index = lax.optimization_barrier((swap_cores(white, freq_count), *index))
    turned, partial = first_pair(white, other, table, width)
    lower, upper, partial = lax.optimization_barrier((lower, upper, partial))
    lower = along_z(lower, hop, chan_count, freq_count)
    upper = along_z(upper, -hop, chan_count, freq_count)
    base = pick(partners, white, lower, upper, top)

    def stage(y_round, y_block, x_block, beside, *operands):
        def make(y_mask, x_mask):
            def run(y_block, x_block, *operands):
                return (
                    exchange(y_block, y_mask * NEAR, chan_count),
                    exchange(x_block, x_mask, chan_count),
                    beside(*operands),
                )

            return run

        return lax.switch(
            index[y_round],
            [make(i, j) for i in range(y_count) for j in range(NEAR)],
            y_block,
            x_block,
            *operands,
        )

    half_0, half_1, _ = stage(0, base[0], base[1], lambda: ())
    kept, passing = beside_step(partial, freq_count)
    half_0, half_1, kept, passing = lax.optimization_barrier((half_0, half_1, kept, passing))
    block_1, half_2, sum_own = stage(
        1, half_1, base[2], lambda *sums: across_step(*sums, freq_count), kept, passing
    )
    partial = next_pairs(turned, block_1, swap_cores(block_1, freq_count))
    block_2, block_0, step_1 = stage(
        2, half_2, half_0, lambda partial: beside_step(partial, freq_count), partial
    )
    sum_1 = across_step(*step_1, freq_count)
    other_0, other_2 = swap_cores(block_0, freq_count), swap_cores(block_2, freq_count)
    sum_02 = scatter(next_pairs(turned, block_0, other_0, block_2, other_2), freq_count)
    return jnp.concatenate([sum_own, sum_02[:1], sum_1, sum_02[1:]])[None]


def solution(mesh):
    return jax.shard_map(
        shards,
        mesh=mesh,
        in_specs=(P("chan", "freq", None), P("chan"), P()),
        out_specs=P("freq", None, "chan", None),
        check_vma=False,
    )
```

```python
import functools

import jax
import jax.numpy as jnp
import numpy as np
from jax import lax
from jax.experimental import pallas as pl
from jax.experimental.pallas import tpu as pltpu
from jax.sharding import PartitionSpec as P

HMAX = 4
ROUNDS = 3
CORES = 2
ROWS = 16
ORDER = (0, 2, 1, 3)
NEAR = 4


def tables(freq_count, bin_dev, seg_count):
    chips = freq_count // CORES
    bin_count = freq_count * bin_dev
    out = np.zeros((freq_count, 2 * chips, CORES * bin_dev, 2 * seg_count), np.float32)
    sign = np.where(np.arange(2 * seg_count) < seg_count, -1.0, 1.0)
    for index in range(freq_count):
        chip, core = index // CORES, index % CORES
        bins = np.concatenate(
            [index * bin_dev + np.arange(bin_dev), (index ^ 1) * bin_dev + np.arange(bin_dev)]
        )
        for d in range(chips):
            lag = (chip ^ ORDER[d]) * CORES + core
            theta = 2.0 * np.pi * ((bins * lag) % bin_count) / bin_count
            factor = 1.0 / np.sqrt(seg_count * bin_count)
            out[index, d] = np.cos(theta)[:, None] * factor
            out[index, chips + d] = np.sin(theta)[:, None] * factor * sign
    return out.reshape(freq_count, 2 * chips, -1)


def whiten_kernel(bin_dev, width, x_ref, low_ref, high_ref, half_ref, out_ref):
    half = width // 2

    def block(ref, rows, index):
        return ref[rows, index * width : (index + 1) * width].astype(jnp.float32)

    def step(i, carry):
        rows = pl.ds(pl.multiple_of(i * ROWS, ROWS), ROWS)
        own = [block(x_ref, rows, g) for g in range(bin_dev)]
        wide = [block(low_ref, rows, g) for g in range(HMAX)]
        wide += own
        wide += [block(high_ref, rows, g) for g in range(HMAX)]
        power = []
        for value in wide:
            square = value * value
            power.append(square + pltpu.roll(square, half, 1))
        hw = half_ref[rows, :]
        scale = 1.0 / (2.0 * hw + 1.0)
        for g in range(bin_dev):
            centre = g + HMAX
            total = power[centre]
            for k in range(1, HMAX + 1):
                both = power[centre - k] + power[centre + k]
                total = total + (both if k == 1 else jnp.where(hw >= k, both, 0.0))
            smooth = jnp.maximum(total * scale, 0.5)
            out_ref[rows, g * width : (g + 1) * width] = (own[g] * lax.rsqrt(smooth)).astype(
                jnp.bfloat16
            )
        return carry

    lax.fori_loop(0, x_ref.shape[0] // ROWS, step, 0)


def whiten(x, low, high, half_wide, bin_dev):
    return pl.pallas_call(
        functools.partial(whiten_kernel, bin_dev, x.shape[1] // bin_dev),
        out_shape=jax.ShapeDtypeStruct(x.shape, jnp.bfloat16),
        compiler_params=pltpu.CompilerParams(vmem_limit_bytes=16 << 20),
        name="whiten",
    )(x, low, high, half_wide)


NT = (((1,), (1,)), ((), ()))


def correlate(turned_ref, blocks, out_ref):
    def step(d, carry):
        for j, (mine_ref, other_ref) in enumerate(blocks):
            span = mine_ref.shape[1]
            total = lax.dot_general(
                turned_ref[d, :, :span], mine_ref[...], NT, preferred_element_type=jnp.float32
            )
            total += lax.dot_general(
                turned_ref[d, :, span:], other_ref[...], NT, preferred_element_type=jnp.float32
            )
            out_ref[d, j] = total.astype(jnp.bfloat16)
        return carry

    lax.fori_loop(0, turned_ref.shape[0], step, 0)


def first_kernel(width, mine_ref, other_ref, table_ref, turned_ref, out_ref):
    rows_all, span = mine_ref.shape
    chips = turned_ref.shape[0]
    for part, ref in enumerate((mine_ref, other_ref)):

        def turn(g, carry, part=part, ref=ref):
            lanes = pl.ds(pl.multiple_of(g * width, width), width)
            to = pl.ds(pl.multiple_of(part * span + g * width, width), width)
            wide = [jnp.broadcast_to(table_ref[k : k + 1, to], (ROWS, width)) for k in range(2 * chips)]

            def step(i, inner):
                rows = pl.ds(pl.multiple_of(i * ROWS, ROWS), ROWS)
                value = ref[rows, lanes].astype(jnp.float32)
                swapped = pltpu.roll(value, width // 2, 1)
                for d in range(chips):
                    turned_ref[d, rows, to] = (value * wide[d] + swapped * wide[chips + d]).astype(
                        jnp.bfloat16
                    )
                return inner

            return lax.fori_loop(0, rows_all // ROWS, step, carry, unroll=8)

        lax.fori_loop(0, span // width, turn, 0)
    correlate(turned_ref, [(mine_ref, other_ref)], out_ref)


def first_pair(mine, other, table, width):
    rows, span = mine.shape
    chips = table.shape[0] // 2
    return pl.pallas_call(
        functools.partial(first_kernel, width),
        out_shape=[
            jax.ShapeDtypeStruct((chips, rows, 2 * span), jnp.bfloat16),
            jax.ShapeDtypeStruct((chips, 1, rows, rows), jnp.bfloat16),
        ],
        compiler_params=pltpu.CompilerParams(vmem_limit_bytes=20 << 20),
        name="first_pair",
    )(mine, other, table)


def pairs_kernel(turned_ref, *refs):
    correlate(turned_ref, list(zip(refs[:-1:2], refs[1:-1:2])), refs[-1])


def next_pairs(turned, *halves):
    rows = halves[0].shape[0]
    return pl.pallas_call(
        pairs_kernel,
        out_shape=jax.ShapeDtypeStruct(
            (turned.shape[0], len(halves) // 2, rows, rows), jnp.bfloat16
        ),
        compiler_params=pltpu.CompilerParams(vmem_limit_bytes=20 << 20),
        cost_estimate=pl.CostEstimate(
            flops=2 * len(halves) * turned.size * rows, bytes_accessed=2 * turned.size, transcendentals=0
        ),
        name="next_pairs",
    )(turned, *halves)


def swap_cores(block, size):
    return lax.ppermute(block, "freq", [(i, i ^ 1) for i in range(size)])


def beside_step(partial, size):
    half = partial.shape[0] // 2
    route = [(i, i ^ CORES) for i in range(size)]
    arrived = lax.ppermute(partial[half:], "freq", route).astype(jnp.float32)
    passing = (partial[1].astype(jnp.float32) + arrived[1]).astype(jnp.bfloat16)
    return partial[0].astype(jnp.float32) + arrived[0], passing


def across_step(kept, passing, size):
    route = [(i, i ^ (2 * CORES)) for i in range(size)]
    passed = lax.ppermute(passing, "freq", route).astype(jnp.float32)
    return (kept + passed).astype(jnp.bfloat16)


def scatter(partial, size):
    return across_step(*beside_step(partial, size), size)


def exchange(block, mask, count):
    if mask == 0:
        return block
    return lax.ppermute(block, "chan", [(i, i ^ mask) for i in range(count)])


def pick_kernel(top, mask_ref, own, far, *refs):
    outs, sems = refs[:-1], refs[-1]
    for r, out in enumerate(outs):
        high = mask_ref[r, 0] & top

        @pl.when(high == 0)
        def _(out=out, r=r):
            pltpu.make_async_copy(own, out, sems.at[r]).start()

        @pl.when(high != 0)
        def _(out=out, r=r):
            pltpu.make_async_copy(far, out, sems.at[r]).start()

    for r, out in enumerate(outs):
        pltpu.make_async_copy(own, out, sems.at[r]).wait()


def pick(partners, own, far, top):
    return pl.pallas_call(
        functools.partial(pick_kernel, top),
        in_specs=[pl.BlockSpec(memory_space=pltpu.SMEM)] + [pl.BlockSpec(memory_space=pl.ANY)] * 2,
        out_specs=[pl.BlockSpec(memory_space=pl.ANY)] * ROUNDS,
        out_shape=[jax.ShapeDtypeStruct(own.shape, own.dtype)] * ROUNDS,
        scratch_shapes=[pltpu.SemaphoreType.DMA((ROUNDS,))],
        compiler_params=pltpu.CompilerParams(vmem_limit_bytes=1 << 20),
        name="pick",
    )(partners, own, far)


def shards(spectra, half_width, partners):
    freq_count = lax.axis_size("freq")
    chan_count = lax.axis_size("chan")
    channels, bin_dev, width = spectra.shape
    x = spectra.reshape(channels, bin_dev * width)
    edge = HMAX * width
    up = [(i, i + 1) for i in range(freq_count - 1)]
    down = [(i + 1, i) for i in range(freq_count - 1)]
    low = lax.ppermute(x[:, -edge:], "freq", up)
    high = lax.ppermute(x[:, :edge], "freq", down)
    half_wide = jnp.broadcast_to(half_width.astype(jnp.float32)[:, None], (channels, width))
    table = lax.dynamic_index_in_dim(
        jnp.asarray(tables(freq_count, bin_dev, width // 2)),
        lax.axis_index("freq"),
        0,
        keepdims=False,
    )
    white = whiten(x, low, high, half_wide, bin_dev)
    top = chan_count // 2
    y_count = top // NEAR
    masks = partners[:, 0]
    x_of, y_of = masks & (NEAR - 1), (masks & (top - 1)) >> (NEAR.bit_length() - 1)
    index = [y_of[r] * NEAR + x_of[(r + 1) % ROUNDS] for r in range(ROUNDS)]
    far_white = exchange(white, top, chan_count)
    other, *index = lax.optimization_barrier((swap_cores(white, freq_count), *index))
    turned, partial = first_pair(white, other, table, width)
    far_white, partial = lax.optimization_barrier((far_white, partial))
    base = pick(partners, white, far_white, top)

    def stage(y_round, y_block, x_block, beside, *operands):
        def make(y_mask, x_mask):
            def run(y_block, x_block, *operands):
                return (
                    exchange(y_block, y_mask * NEAR, chan_count),
                    exchange(x_block, x_mask, chan_count),
                    beside(*operands),
                )

            return run

        return lax.switch(
            index[y_round],
            [make(i, j) for i in range(y_count) for j in range(NEAR)],
            y_block,
            x_block,
            *operands,
        )

    half_0, half_1, _ = stage(0, base[0], base[1], lambda: ())
    kept, passing = beside_step(partial, freq_count)
    half_0, half_1, kept, passing = lax.optimization_barrier((half_0, half_1, kept, passing))
    block_1, half_2, sum_own = stage(
        1, half_1, base[2], lambda *sums: across_step(*sums, freq_count), kept, passing
    )
    block_2, block_0, other_1 = stage(
        2, half_2, half_0, lambda block: swap_cores(block, freq_count), block_1
    )
    partial = next_pairs(turned, block_1, other_1)
    block_0, block_2, partial = lax.optimization_barrier((block_0, block_2, partial))
    step_1 = beside_step(partial, freq_count)
    other_0, other_2 = swap_cores(block_0, freq_count), swap_cores(block_2, freq_count)
    other_0, other_2, *step_1 = lax.optimization_barrier((other_0, other_2, *step_1))
    sum_1 = across_step(*step_1, freq_count)
    partial = next_pairs(turned, block_0, other_0, block_2, other_2)
    *step_02, sum_1 = lax.optimization_barrier((*beside_step(partial, freq_count), sum_1))
    sum_02 = across_step(*step_02, freq_count)
    return jnp.concatenate([sum_own, sum_02[:1], sum_1, sum_02[1:]])[None]


def solution(mesh):
    return jax.shard_map(
        shards,
        mesh=mesh,
        in_specs=(P("chan", "freq", None), P("chan"), P()),
        out_specs=P("freq", None, "chan", None),
        check_vma=False,
    )
```

```python
import functools

import jax
import jax.numpy as jnp
import numpy as np
from jax import lax
from jax.experimental import pallas as pl
from jax.experimental.pallas import tpu as pltpu
from jax.sharding import PartitionSpec as P

HMAX = 4
ROUNDS = 3
CORES = 2
ROWS = 16
ORDER = (0, 2, 1, 3)
NEAR = 4


def tables(freq_count, bin_dev, seg_count):
    chips = freq_count // CORES
    bin_count = freq_count * bin_dev
    out = np.zeros((freq_count, 2 * chips, CORES * bin_dev, 2 * seg_count), np.float32)
    sign = np.where(np.arange(2 * seg_count) < seg_count, -1.0, 1.0)
    for index in range(freq_count):
        chip, core = index // CORES, index % CORES
        bins = np.concatenate(
            [index * bin_dev + np.arange(bin_dev), (index ^ 1) * bin_dev + np.arange(bin_dev)]
        )
        for d in range(chips):
            lag = (chip ^ ORDER[d]) * CORES + core
            theta = 2.0 * np.pi * ((bins * lag) % bin_count) / bin_count
            factor = 1.0 / np.sqrt(seg_count * bin_count)
            out[index, d] = np.cos(theta)[:, None] * factor
            out[index, chips + d] = np.sin(theta)[:, None] * factor * sign
    return out.reshape(freq_count, 2 * chips, -1)


def whiten_kernel(bin_dev, width, x_ref, low_ref, high_ref, half_ref, out_ref):
    half = width // 2

    def block(ref, rows, index):
        return ref[rows, index * width : (index + 1) * width].astype(jnp.float32)

    def step(i, carry):
        rows = pl.ds(pl.multiple_of(i * ROWS, ROWS), ROWS)
        own = [block(x_ref, rows, g) for g in range(bin_dev)]
        wide = [block(low_ref, rows, g) for g in range(HMAX)]
        wide += own
        wide += [block(high_ref, rows, g) for g in range(HMAX)]
        power = []
        for value in wide:
            square = value * value
            power.append(square + pltpu.roll(square, half, 1))
        hw = half_ref[rows, :]
        scale = 1.0 / (2.0 * hw + 1.0)
        for g in range(bin_dev):
            centre = g + HMAX
            total = power[centre]
            for k in range(1, HMAX + 1):
                both = power[centre - k] + power[centre + k]
                total = total + (both if k == 1 else jnp.where(hw >= k, both, 0.0))
            smooth = jnp.maximum(total * scale, 0.5)
            out_ref[rows, g * width : (g + 1) * width] = (own[g] * lax.rsqrt(smooth)).astype(
                jnp.bfloat16
            )
        return carry

    lax.fori_loop(0, x_ref.shape[0] // ROWS, step, 0)


def whiten(x, low, high, half_wide, bin_dev):
    return pl.pallas_call(
        functools.partial(whiten_kernel, bin_dev, x.shape[1] // bin_dev),
        out_shape=jax.ShapeDtypeStruct(x.shape, jnp.bfloat16),
        compiler_params=pltpu.CompilerParams(vmem_limit_bytes=16 << 20),
        name="whiten",
    )(x, low, high, half_wide)


NT = (((1,), (1,)), ((), ()))


def correlate(turned_ref, blocks, out_ref):
    def step(d, carry):
        for j, (mine_ref, other_ref) in enumerate(blocks):
            span = mine_ref.shape[1]
            total = lax.dot_general(
                turned_ref[d, :, :span], mine_ref[...], NT, preferred_element_type=jnp.float32
            )
            total += lax.dot_general(
                turned_ref[d, :, span:], other_ref[...], NT, preferred_element_type=jnp.float32
            )
            out_ref[d, j] = total.astype(jnp.bfloat16)
        return carry

    lax.fori_loop(0, turned_ref.shape[0], step, 0)


def first_kernel(width, mine_ref, other_ref, table_ref, turned_ref, out_ref):
    rows_all, span = mine_ref.shape
    chips = turned_ref.shape[0]
    for part, ref in enumerate((mine_ref, other_ref)):

        def turn(g, carry, part=part, ref=ref):
            lanes = pl.ds(pl.multiple_of(g * width, width), width)
            to = pl.ds(pl.multiple_of(part * span + g * width, width), width)
            wide = [jnp.broadcast_to(table_ref[k : k + 1, to], (ROWS, width)) for k in range(2 * chips)]

            def step(i, inner):
                rows = pl.ds(pl.multiple_of(i * ROWS, ROWS), ROWS)
                value = ref[rows, lanes].astype(jnp.float32)
                swapped = pltpu.roll(value, width // 2, 1)
                for d in range(chips):
                    turned_ref[d, rows, to] = (value * wide[d] + swapped * wide[chips + d]).astype(
                        jnp.bfloat16
                    )
                return inner

            return lax.fori_loop(0, rows_all // ROWS, step, carry, unroll=8)

        lax.fori_loop(0, span // width, turn, 0)
    correlate(turned_ref, [(mine_ref, other_ref)], out_ref)


def first_pair(mine, other, table, width):
    rows, span = mine.shape
    chips = table.shape[0] // 2
    return pl.pallas_call(
        functools.partial(first_kernel, width),
        out_shape=[
            jax.ShapeDtypeStruct((chips, rows, 2 * span), jnp.bfloat16),
            jax.ShapeDtypeStruct((chips, 1, rows, rows), jnp.bfloat16),
        ],
        compiler_params=pltpu.CompilerParams(vmem_limit_bytes=20 << 20),
        name="first_pair",
    )(mine, other, table)


def pairs_kernel(turned_ref, *refs):
    correlate(turned_ref, list(zip(refs[:-1:2], refs[1:-1:2])), refs[-1])


def next_pairs(turned, *halves):
    rows = halves[0].shape[0]
    return pl.pallas_call(
        pairs_kernel,
        out_shape=jax.ShapeDtypeStruct(
            (turned.shape[0], len(halves) // 2, rows, rows), jnp.bfloat16
        ),
        compiler_params=pltpu.CompilerParams(vmem_limit_bytes=20 << 20),
        cost_estimate=pl.CostEstimate(
            flops=2 * len(halves) * turned.size * rows, bytes_accessed=2 * turned.size, transcendentals=0
        ),
        name="next_pairs",
    )(turned, *halves)


def swap_cores(block, size):
    return lax.ppermute(block, "freq", [(i, i ^ 1) for i in range(size)])


def beside_step(partial, size):
    half = partial.shape[0] // 2
    route = [(i, i ^ CORES) for i in range(size)]
    arrived = lax.ppermute(partial[half:], "freq", route).astype(jnp.float32)
    passing = (partial[1].astype(jnp.float32) + arrived[1]).astype(jnp.bfloat16)
    return partial[0].astype(jnp.float32) + arrived[0], passing


def across_step(kept, passing, size):
    route = [(i, i ^ (2 * CORES)) for i in range(size)]
    passed = lax.ppermute(passing, "freq", route).astype(jnp.float32)
    return (kept + passed).astype(jnp.bfloat16)


def scatter(partial, size):
    return across_step(*beside_step(partial, size), size)


def exchange(block, mask, count):
    if mask == 0:
        return block
    return lax.ppermute(block, "chan", [(i, i ^ mask) for i in range(count)])


def pick_kernel(top, mask_ref, own, far, *refs):
    outs, sems = refs[:-1], refs[-1]
    for r, out in enumerate(outs):
        high = mask_ref[r, 0] & top

        @pl.when(high == 0)
        def _(out=out, r=r):
            pltpu.make_async_copy(own, out, sems.at[r]).start()

        @pl.when(high != 0)
        def _(out=out, r=r):
            pltpu.make_async_copy(far, out, sems.at[r]).start()

    for r, out in enumerate(outs):
        pltpu.make_async_copy(own, out, sems.at[r]).wait()


def pick(partners, own, far, top):
    return pl.pallas_call(
        functools.partial(pick_kernel, top),
        in_specs=[pl.BlockSpec(memory_space=pltpu.SMEM)] + [pl.BlockSpec(memory_space=pl.ANY)] * 2,
        out_specs=[pl.BlockSpec(memory_space=pl.ANY)] * ROUNDS,
        out_shape=[jax.ShapeDtypeStruct(own.shape, own.dtype)] * ROUNDS,
        scratch_shapes=[pltpu.SemaphoreType.DMA((ROUNDS,))],
        compiler_params=pltpu.CompilerParams(vmem_limit_bytes=1 << 20),
        name="pick",
    )(partners, own, far)


def shards(spectra, half_width, partners):
    freq_count = lax.axis_size("freq")
    chan_count = lax.axis_size("chan")
    channels, bin_dev, width = spectra.shape
    x = spectra.reshape(channels, bin_dev * width)
    edge = HMAX * width
    up = [(i, i + 1) for i in range(freq_count - 1)]
    down = [(i + 1, i) for i in range(freq_count - 1)]
    low = lax.ppermute(x[:, -edge:], "freq", up)
    high = lax.ppermute(x[:, :edge], "freq", down)
    half_wide = jnp.broadcast_to(half_width.astype(jnp.float32)[:, None], (channels, width))
    table = lax.dynamic_index_in_dim(
        jnp.asarray(tables(freq_count, bin_dev, width // 2)),
        lax.axis_index("freq"),
        0,
        keepdims=False,
    )
    white = whiten(x, low, high, half_wide, bin_dev)
    top = chan_count // 2
    y_count = top // NEAR
    masks = partners[:, 0]
    x_of, y_of = masks & (NEAR - 1), (masks & (top - 1)) >> (NEAR.bit_length() - 1)
    index = [y_of[r] * NEAR + x_of[(r + 1) % ROUNDS] for r in range(ROUNDS)]
    far_white = exchange(white, top, chan_count)
    other, *index = lax.optimization_barrier((swap_cores(white, freq_count), *index))
    turned, partial = first_pair(white, other, table, width)
    far_white, partial = lax.optimization_barrier((far_white, partial))
    base = pick(partners, white, far_white, top)

    def stage(y_round, y_block, x_block, beside, *operands):
        def make(y_mask, x_mask):
            def run(y_block, x_block, *operands):
                return (
                    exchange(y_block, y_mask * NEAR, chan_count),
                    exchange(x_block, x_mask, chan_count),
                    beside(*operands),
                )

            return run

        return lax.switch(
            index[y_round],
            [make(i, j) for i in range(y_count) for j in range(NEAR)],
            y_block,
            x_block,
            *operands,
        )

    half_0, half_1, _ = stage(0, base[0], base[1], lambda: ())
    kept, passing = beside_step(partial, freq_count)
    half_0, half_1, kept, passing = lax.optimization_barrier((half_0, half_1, kept, passing))
    block_1, half_2, sum_own = stage(
        1, half_1, base[2], lambda *sums: across_step(*sums, freq_count), kept, passing
    )
    block_2, block_0, other_1 = stage(
        2, half_2, half_0, lambda block: swap_cores(block, freq_count), block_1
    )
    other_0, other_2 = swap_cores(block_0, freq_count), swap_cores(block_2, freq_count)
    partial = next_pairs(turned, block_0, other_0, block_1, other_1, block_2, other_2)
    return jnp.concatenate([sum_own, scatter(partial, freq_count)])[None]


def solution(mesh):
    return jax.shard_map(
        shards,
        mesh=mesh,
        in_specs=(P("chan", "freq", None), P("chan"), P()),
        out_specs=P("freq", None, "chan", None),
        check_vma=False,
    )
```

```python
import functools

import jax
import jax.numpy as jnp
import numpy as np
from jax import lax
from jax.experimental import pallas as pl
from jax.experimental.pallas import tpu as pltpu
from jax.sharding import PartitionSpec as P

HMAX = 4
ROUNDS = 3
CORES = 2
ROWS = 16
ORDER = (0, 2, 1, 3)
NEAR = 4


def tables(freq_count, bin_dev, seg_count):
    chips = freq_count // CORES
    bin_count = freq_count * bin_dev
    out = np.zeros((freq_count, 2 * chips, CORES * bin_dev, 2 * seg_count), np.float32)
    sign = np.where(np.arange(2 * seg_count) < seg_count, -1.0, 1.0)
    for index in range(freq_count):
        chip, core = index // CORES, index % CORES
        bins = np.concatenate(
            [index * bin_dev + np.arange(bin_dev), (index ^ 1) * bin_dev + np.arange(bin_dev)]
        )
        for d in range(chips):
            lag = (chip ^ ORDER[d]) * CORES + core
            theta = 2.0 * np.pi * ((bins * lag) % bin_count) / bin_count
            factor = 1.0 / np.sqrt(seg_count * bin_count)
            out[index, d] = np.cos(theta)[:, None] * factor
            out[index, chips + d] = np.sin(theta)[:, None] * factor * sign
    return out.reshape(freq_count, 2 * chips, -1)


def whiten_kernel(bin_dev, width, x_ref, low_ref, high_ref, half_ref, out_ref):
    half = width // 2

    def block(ref, rows, index):
        return ref[rows, index * width : (index + 1) * width].astype(jnp.float32)

    def step(i, carry):
        rows = pl.ds(pl.multiple_of(i * ROWS, ROWS), ROWS)
        own = [block(x_ref, rows, g) for g in range(bin_dev)]
        wide = [block(low_ref, rows, g) for g in range(HMAX)]
        wide += own
        wide += [block(high_ref, rows, g) for g in range(HMAX)]
        power = []
        for value in wide:
            square = value * value
            power.append(square + pltpu.roll(square, half, 1))
        hw = half_ref[rows, :]
        scale = 1.0 / (2.0 * hw + 1.0)
        for g in range(bin_dev):
            centre = g + HMAX
            total = power[centre]
            for k in range(1, HMAX + 1):
                both = power[centre - k] + power[centre + k]
                total = total + (both if k == 1 else jnp.where(hw >= k, both, 0.0))
            smooth = jnp.maximum(total * scale, 0.5)
            out_ref[rows, g * width : (g + 1) * width] = (own[g] * lax.rsqrt(smooth)).astype(
                jnp.bfloat16
            )
        return carry

    lax.fori_loop(0, x_ref.shape[0] // ROWS, step, 0)


def whiten(x, low, high, half_wide, bin_dev):
    return pl.pallas_call(
        functools.partial(whiten_kernel, bin_dev, x.shape[1] // bin_dev),
        out_shape=jax.ShapeDtypeStruct(x.shape, jnp.bfloat16),
        compiler_params=pltpu.CompilerParams(vmem_limit_bytes=16 << 20),
        name="whiten",
    )(x, low, high, half_wide)


NT = (((1,), (1,)), ((), ()))


def correlate(turned_ref, blocks, out_ref):
    def step(d, carry):
        for j, (mine_ref, other_ref) in enumerate(blocks):
            span = mine_ref.shape[1]
            total = lax.dot_general(
                turned_ref[d, :, :span], mine_ref[...], NT, preferred_element_type=jnp.float32
            )
            total += lax.dot_general(
                turned_ref[d, :, span:], other_ref[...], NT, preferred_element_type=jnp.float32
            )
            out_ref[d, j] = total.astype(jnp.bfloat16)
        return carry

    lax.fori_loop(0, turned_ref.shape[0], step, 0)


def first_kernel(width, mine_ref, other_ref, table_ref, turned_ref, out_ref):
    rows_all, span = mine_ref.shape
    chips = turned_ref.shape[0]
    for part, ref in enumerate((mine_ref, other_ref)):

        def turn(g, carry, part=part, ref=ref):
            lanes = pl.ds(pl.multiple_of(g * width, width), width)
            to = pl.ds(pl.multiple_of(part * span + g * width, width), width)
            wide = [jnp.broadcast_to(table_ref[k : k + 1, to], (ROWS, width)) for k in range(2 * chips)]

            def step(i, inner):
                rows = pl.ds(pl.multiple_of(i * ROWS, ROWS), ROWS)
                value = ref[rows, lanes].astype(jnp.float32)
                swapped = pltpu.roll(value, width // 2, 1)
                for d in range(chips):
                    turned_ref[d, rows, to] = (value * wide[d] + swapped * wide[chips + d]).astype(
                        jnp.bfloat16
                    )
                return inner

            return lax.fori_loop(0, rows_all // ROWS, step, carry, unroll=8)

        lax.fori_loop(0, span // width, turn, 0)
    correlate(turned_ref, [(mine_ref, other_ref)], out_ref)


def first_pair(mine, other, table, width):
    rows, span = mine.shape
    chips = table.shape[0] // 2
    return pl.pallas_call(
        functools.partial(first_kernel, width),
        out_shape=[
            jax.ShapeDtypeStruct((chips, rows, 2 * span), jnp.bfloat16),
            jax.ShapeDtypeStruct((chips, 1, rows, rows), jnp.bfloat16),
        ],
        compiler_params=pltpu.CompilerParams(vmem_limit_bytes=20 << 20),
        name="first_pair",
    )(mine, other, table)


def pairs_kernel(turned_ref, *refs):
    correlate(turned_ref, list(zip(refs[:-1:2], refs[1:-1:2])), refs[-1])


def next_pairs(turned, *halves):
    rows = halves[0].shape[0]
    return pl.pallas_call(
        pairs_kernel,
        out_shape=jax.ShapeDtypeStruct(
            (turned.shape[0], len(halves) // 2, rows, rows), jnp.bfloat16
        ),
        compiler_params=pltpu.CompilerParams(vmem_limit_bytes=20 << 20),
        cost_estimate=pl.CostEstimate(
            flops=2 * len(halves) * turned.size * rows, bytes_accessed=2 * turned.size, transcendentals=0
        ),
        name="next_pairs",
    )(turned, *halves)


def swap_cores(block, size):
    return lax.ppermute(block, "freq", [(i, i ^ 1) for i in range(size)])


def beside_step(partial, size):
    half = partial.shape[0] // 2
    route = [(i, i ^ CORES) for i in range(size)]
    arrived = lax.ppermute(partial[half:], "freq", route).astype(jnp.float32)
    passing = (partial[1].astype(jnp.float32) + arrived[1]).astype(jnp.bfloat16)
    return partial[0].astype(jnp.float32) + arrived[0], passing


def across_step(kept, passing, size):
    route = [(i, i ^ (2 * CORES)) for i in range(size)]
    passed = lax.ppermute(passing, "freq", route).astype(jnp.float32)
    return (kept + passed).astype(jnp.bfloat16)


def scatter(partial, size):
    total = partial[0].astype(jnp.float32)
    for k in range(1, partial.shape[0]):
        route = [(i, i ^ (ORDER[k] * CORES)) for i in range(size)]
        total = total + lax.ppermute(partial[k], "freq", route).astype(jnp.float32)
    return total.astype(jnp.bfloat16)


def exchange(block, mask, count):
    if mask == 0:
        return block
    return lax.ppermute(block, "chan", [(i, i ^ mask) for i in range(count)])


def pick_kernel(top, mask_ref, own, far, *refs):
    outs, sems = refs[:-1], refs[-1]
    for r, out in enumerate(outs):
        high = mask_ref[r, 0] & top

        @pl.when(high == 0)
        def _(out=out, r=r):
            pltpu.make_async_copy(own, out, sems.at[r]).start()

        @pl.when(high != 0)
        def _(out=out, r=r):
            pltpu.make_async_copy(far, out, sems.at[r]).start()

    for r, out in enumerate(outs):
        pltpu.make_async_copy(own, out, sems.at[r]).wait()


def pick(partners, own, far, top):
    return pl.pallas_call(
        functools.partial(pick_kernel, top),
        in_specs=[pl.BlockSpec(memory_space=pltpu.SMEM)] + [pl.BlockSpec(memory_space=pl.ANY)] * 2,
        out_specs=[pl.BlockSpec(memory_space=pl.ANY)] * ROUNDS,
        out_shape=[jax.ShapeDtypeStruct(own.shape, own.dtype)] * ROUNDS,
        scratch_shapes=[pltpu.SemaphoreType.DMA((ROUNDS,))],
        compiler_params=pltpu.CompilerParams(vmem_limit_bytes=1 << 20),
        name="pick",
    )(partners, own, far)


def shards(spectra, half_width, partners):
    freq_count = lax.axis_size("freq")
    chan_count = lax.axis_size("chan")
    channels, bin_dev, width = spectra.shape
    x = spectra.reshape(channels, bin_dev * width)
    edge = HMAX * width
    up = [(i, i + 1) for i in range(freq_count - 1)]
    down = [(i + 1, i) for i in range(freq_count - 1)]
    low = lax.ppermute(x[:, -edge:], "freq", up)
    high = lax.ppermute(x[:, :edge], "freq", down)
    half_wide = jnp.broadcast_to(half_width.astype(jnp.float32)[:, None], (channels, width))
    table = lax.dynamic_index_in_dim(
        jnp.asarray(tables(freq_count, bin_dev, width // 2)),
        lax.axis_index("freq"),
        0,
        keepdims=False,
    )
    white = whiten(x, low, high, half_wide, bin_dev)
    top = chan_count // 2
    y_count = top // NEAR
    masks = partners[:, 0]
    x_of, y_of = masks & (NEAR - 1), (masks & (top - 1)) >> (NEAR.bit_length() - 1)
    index = [y_of[r] * NEAR + x_of[(r + 1) % ROUNDS] for r in range(ROUNDS)]
    far_white = exchange(white, top, chan_count)
    other, *index = lax.optimization_barrier((swap_cores(white, freq_count), *index))
    turned, partial = first_pair(white, other, table, width)
    far_white, partial = lax.optimization_barrier((far_white, partial))
    base = pick(partners, white, far_white, top)

    def stage(y_round, y_block, x_block, beside, *operands):
        def make(y_mask, x_mask):
            def run(y_block, x_block, *operands):
                return (
                    exchange(y_block, y_mask * NEAR, chan_count),
                    exchange(x_block, x_mask, chan_count),
                    beside(*operands),
                )

            return run

        return lax.switch(
            index[y_round],
            [make(i, j) for i in range(y_count) for j in range(NEAR)],
            y_block,
            x_block,
            *operands,
        )

    half_0, half_1, _ = stage(0, base[0], base[1], lambda: ())
    kept, passing = beside_step(partial, freq_count)
    half_0, half_1, kept, passing = lax.optimization_barrier((half_0, half_1, kept, passing))
    block_1, half_2, sum_own = stage(
        1, half_1, base[2], lambda *sums: across_step(*sums, freq_count), kept, passing
    )
    block_2, block_0, other_1 = stage(
        2, half_2, half_0, lambda block: swap_cores(block, freq_count), block_1
    )
    other_0, other_2 = swap_cores(block_0, freq_count), swap_cores(block_2, freq_count)
    partial = next_pairs(turned, block_0, other_0, block_1, other_1, block_2, other_2)
    return jnp.concatenate([sum_own, scatter(partial, freq_count)])[None]


def solution(mesh):
    return jax.shard_map(
        shards,
        mesh=mesh,
        in_specs=(P("chan", "freq", None), P("chan"), P()),
        out_specs=P("freq", None, "chan", None),
        check_vma=False,
    )
```

```python
import functools

import jax
import jax.numpy as jnp
import numpy as np
from jax import lax
from jax.experimental import pallas as pl
from jax.experimental.pallas import tpu as pltpu
from jax.sharding import PartitionSpec as P

HMAX = 4
ROUNDS = 3
CORES = 2
ROWS = 16
ORDER = (0, 2, 1, 3)
NEAR = 4


def tables(freq_count, bin_dev, seg_count):
    chips = freq_count // CORES
    bin_count = freq_count * bin_dev
    out = np.zeros((freq_count, 2 * chips, CORES * bin_dev, 2 * seg_count), np.float32)
    sign = np.where(np.arange(2 * seg_count) < seg_count, -1.0, 1.0)
    for index in range(freq_count):
        chip, core = index // CORES, index % CORES
        bins = np.concatenate(
            [index * bin_dev + np.arange(bin_dev), (index ^ 1) * bin_dev + np.arange(bin_dev)]
        )
        for d in range(chips):
            lag = (chip ^ ORDER[d]) * CORES + core
            theta = 2.0 * np.pi * ((bins * lag) % bin_count) / bin_count
            factor = 1.0 / np.sqrt(seg_count * bin_count)
            out[index, d] = np.cos(theta)[:, None] * factor
            out[index, chips + d] = np.sin(theta)[:, None] * factor * sign
    return out.reshape(freq_count, 2 * chips, -1)


def whiten_kernel(bin_dev, width, x_ref, low_ref, high_ref, half_ref, out_ref):
    half = width // 2

    def block(ref, rows, index):
        return ref[rows, index * width : (index + 1) * width].astype(jnp.float32)

    def step(i, carry):
        rows = pl.ds(pl.multiple_of(i * ROWS, ROWS), ROWS)
        own = [block(x_ref, rows, g) for g in range(bin_dev)]
        wide = [block(low_ref, rows, g) for g in range(HMAX)]
        wide += own
        wide += [block(high_ref, rows, g) for g in range(HMAX)]
        power = []
        for value in wide:
            square = value * value
            power.append(square + pltpu.roll(square, half, 1))
        hw = half_ref[rows, :]
        scale = 1.0 / (2.0 * hw + 1.0)
        for g in range(bin_dev):
            centre = g + HMAX
            total = power[centre]
            for k in range(1, HMAX + 1):
                both = power[centre - k] + power[centre + k]
                total = total + (both if k == 1 else jnp.where(hw >= k, both, 0.0))
            smooth = jnp.maximum(total * scale, 0.5)
            out_ref[rows, g * width : (g + 1) * width] = (own[g] * lax.rsqrt(smooth)).astype(
                jnp.bfloat16
            )
        return carry

    lax.fori_loop(0, x_ref.shape[0] // ROWS, step, 0)


def whiten(x, low, high, half_wide, bin_dev):
    return pl.pallas_call(
        functools.partial(whiten_kernel, bin_dev, x.shape[1] // bin_dev),
        out_shape=jax.ShapeDtypeStruct(x.shape, jnp.bfloat16),
        compiler_params=pltpu.CompilerParams(vmem_limit_bytes=16 << 20),
        name="whiten",
    )(x, low, high, half_wide)


NT = (((1,), (1,)), ((), ()))


def correlate(turned_ref, blocks, out_ref):
    def step(d, carry):
        for j, (mine_ref, other_ref) in enumerate(blocks):
            span = mine_ref.shape[1]
            total = lax.dot_general(
                turned_ref[d, :, :span], mine_ref[...], NT, preferred_element_type=jnp.float32
            )
            total += lax.dot_general(
                turned_ref[d, :, span:], other_ref[...], NT, preferred_element_type=jnp.float32
            )
            out_ref[d, j] = total.astype(jnp.bfloat16)
        return carry

    lax.fori_loop(0, turned_ref.shape[0], step, 0)


def first_kernel(width, mine_ref, other_ref, table_ref, turned_ref, out_ref):
    rows_all, span = mine_ref.shape
    chips = turned_ref.shape[0]
    for part, ref in enumerate((mine_ref, other_ref)):

        def turn(g, carry, part=part, ref=ref):
            lanes = pl.ds(pl.multiple_of(g * width, width), width)
            to = pl.ds(pl.multiple_of(part * span + g * width, width), width)
            wide = [jnp.broadcast_to(table_ref[k : k + 1, to], (ROWS, width)) for k in range(2 * chips)]

            def step(i, inner):
                rows = pl.ds(pl.multiple_of(i * ROWS, ROWS), ROWS)
                value = ref[rows, lanes].astype(jnp.float32)
                swapped = pltpu.roll(value, width // 2, 1)
                for d in range(chips):
                    turned_ref[d, rows, to] = (value * wide[d] + swapped * wide[chips + d]).astype(
                        jnp.bfloat16
                    )
                return inner

            return lax.fori_loop(0, rows_all // ROWS, step, carry, unroll=8)

        lax.fori_loop(0, span // width, turn, 0)
    correlate(turned_ref, [(mine_ref, other_ref)], out_ref)


def first_pair(mine, other, table, width):
    rows, span = mine.shape
    chips = table.shape[0] // 2
    return pl.pallas_call(
        functools.partial(first_kernel, width),
        out_shape=[
            jax.ShapeDtypeStruct((chips, rows, 2 * span), jnp.bfloat16),
            jax.ShapeDtypeStruct((chips, 1, rows, rows), jnp.bfloat16),
        ],
        compiler_params=pltpu.CompilerParams(vmem_limit_bytes=20 << 20),
        name="first_pair",
    )(mine, other, table)


def pairs_kernel(turned_ref, *refs):
    correlate(turned_ref, list(zip(refs[:-1:2], refs[1:-1:2])), refs[-1])


def next_pairs(turned, *halves):
    rows = halves[0].shape[0]
    return pl.pallas_call(
        pairs_kernel,
        out_shape=jax.ShapeDtypeStruct(
            (turned.shape[0], len(halves) // 2, rows, rows), jnp.bfloat16
        ),
        compiler_params=pltpu.CompilerParams(vmem_limit_bytes=20 << 20),
        cost_estimate=pl.CostEstimate(
            flops=2 * len(halves) * turned.size * rows, bytes_accessed=2 * turned.size, transcendentals=0
        ),
        name="next_pairs",
    )(turned, *halves)


def swap_cores(block, size):
    return lax.ppermute(block, "freq", [(i, i ^ 1) for i in range(size)])


def beside_step(partial, size):
    half = partial.shape[0] // 2
    route = [(i, i ^ CORES) for i in range(size)]
    arrived = lax.ppermute(partial[half:], "freq", route).astype(jnp.float32)
    passing = (partial[1].astype(jnp.float32) + arrived[1]).astype(jnp.bfloat16)
    return partial[0].astype(jnp.float32) + arrived[0], passing


def across_step(kept, passing, size):
    route = [(i, i ^ (2 * CORES)) for i in range(size)]
    passed = lax.ppermute(passing, "freq", route).astype(jnp.float32)
    return (kept + passed).astype(jnp.bfloat16)


def scatter(partial, size):
    total = partial[0].astype(jnp.float32)
    for k in range(1, partial.shape[0]):
        route = [(i, i ^ (ORDER[k] * CORES)) for i in range(size)]
        total = total + lax.ppermute(partial[k], "freq", route).astype(jnp.float32)
    return total.astype(jnp.bfloat16)


def exchange(block, mask, count):
    if mask == 0:
        return block
    return lax.ppermute(block, "chan", [(i, i ^ mask) for i in range(count)])


def pick_kernel(top, mask_ref, own, far, *refs):
    outs, sems = refs[:-1], refs[-1]
    for r, out in enumerate(outs):
        high = mask_ref[r, 0] & top

        @pl.when(high == 0)
        def _(out=out, r=r):
            pltpu.make_async_copy(own, out, sems.at[r]).start()

        @pl.when(high != 0)
        def _(out=out, r=r):
            pltpu.make_async_copy(far, out, sems.at[r]).start()

    for r, out in enumerate(outs):
        pltpu.make_async_copy(own, out, sems.at[r]).wait()


def pick(partners, own, far, top):
    return pl.pallas_call(
        functools.partial(pick_kernel, top),
        in_specs=[pl.BlockSpec(memory_space=pltpu.SMEM)] + [pl.BlockSpec(memory_space=pl.ANY)] * 2,
        out_specs=[pl.BlockSpec(memory_space=pl.ANY)] * ROUNDS,
        out_shape=[jax.ShapeDtypeStruct(own.shape, own.dtype)] * ROUNDS,
        scratch_shapes=[pltpu.SemaphoreType.DMA((ROUNDS,))],
        compiler_params=pltpu.CompilerParams(vmem_limit_bytes=1 << 20),
        name="pick",
    )(partners, own, far)


def shards(spectra, half_width, partners):
    freq_count = lax.axis_size("freq")
    chan_count = lax.axis_size("chan")
    channels, bin_dev, width = spectra.shape
    x = spectra.reshape(channels, bin_dev * width)
    edge = HMAX * width
    up = [(i, i + 1) for i in range(freq_count - 1)]
    down = [(i + 1, i) for i in range(freq_count - 1)]
    low = lax.ppermute(x[:, -edge:], "freq", up)
    high = lax.ppermute(x[:, :edge], "freq", down)
    half_wide = jnp.broadcast_to(half_width.astype(jnp.float32)[:, None], (channels, width))
    table = lax.dynamic_index_in_dim(
        jnp.asarray(tables(freq_count, bin_dev, width // 2)),
        lax.axis_index("freq"),
        0,
        keepdims=False,
    )
    white = whiten(x, low, high, half_wide, bin_dev)
    top = chan_count // 2
    y_count = top // NEAR
    masks = partners[:, 0]
    x_of, y_of = masks & (NEAR - 1), (masks & (top - 1)) >> (NEAR.bit_length() - 1)
    index = [y_of[r] * NEAR + x_of[(r + 1) % ROUNDS] for r in range(ROUNDS)]
    far_white = exchange(white, top, chan_count)
    other, *index = lax.optimization_barrier((swap_cores(white, freq_count), *index))
    turned, partial = first_pair(white, other, table, width)
    far_white, partial = lax.optimization_barrier((far_white, partial))
    base = pick(partners, white, far_white, top)

    def stage(y_round, y_block, x_block, beside, *operands):
        def make(y_mask, x_mask):
            def run(y_block, x_block, *operands):
                return (
                    exchange(y_block, y_mask * NEAR, chan_count),
                    exchange(x_block, x_mask, chan_count),
                    beside(*operands),
                )

            return run

        return lax.switch(
            index[y_round],
            [make(i, j) for i in range(y_count) for j in range(NEAR)],
            y_block,
            x_block,
            *operands,
        )

    half_0, half_1, own_step = stage(
        0, base[0], base[1], lambda partial: beside_step(partial, freq_count), partial
    )
    block_1, half_2, sum_own = stage(
        1, half_1, base[2], lambda *sums: across_step(*sums, freq_count), *own_step
    )
    block_2, block_0, other_1 = stage(
        2, half_2, half_0, lambda block: swap_cores(block, freq_count), block_1
    )
    other_0, other_2 = swap_cores(block_0, freq_count), swap_cores(block_2, freq_count)
    partial = next_pairs(turned, block_0, other_0, block_1, other_1, block_2, other_2)
    return jnp.concatenate([sum_own, scatter(partial, freq_count)])[None]


def solution(mesh):
    return jax.shard_map(
        shards,
        mesh=mesh,
        in_specs=(P("chan", "freq", None), P("chan"), P()),
        out_specs=P("freq", None, "chan", None),
        check_vma=False,
    )
```
